32 devices in a mesh: gx: 4 (over y, x), gy: 4 (over z), mode: 2 (over core).
Axes of the slice: x: 2, y: 2, z: 4, core: 2. Of those that a mesh axis runs over, the one named last changes fastest.
Arguments:
- state: float32 [4, 64, 128, 1024], P(None, None, 'gx', ('gy', 'mode')), may hold values from -6 to 6
- depth_class: int32 [128, 1024], P('gx', ('gy', 'mode')), may hold values from 0 to 4
- vertical_inverse: float32 [4, 64, 64], replicated, as said below
- height: float32 [128, 1024], P('gx', ('gy', 'mode')), may hold values from -4 to 4
- transport: float32 [2, 128, 1024], P(None, 'gx', ('gy', 'mode')), may hold values from -4 to 4
Outputs:
- state_next: float32 [4, 64, 128, 1024], P(None, None, 'gx', ('gy', 'mode'))
- height_next: float32 [128, 1024], P('gx', ('gy', 'mode'))
- transport_next: float32 [2, 128, 1024], P(None, 'gx', ('gy', 'mode'))
The draws below stay inside these ranges and needn't reach their ends.
Inputs may be any that keep to these rules, and one draw needn't show every extreme that they name: `depth_class`: 0 marks land; a column of class c has its top c * 16 levels active. `vertical_inverse`: entry c is used for columns of class c + 1 and acts on all 64 levels.
All inputs are finite; a program needn't handle non-finite values.
Results may differ from the reference program's by a relative error of at most 0.0003.
Values sent between devices are 32-bit elements; how exact they have to be, the bound alone decides.
A program may use at most 128 MiB of HBM per device.

```python
import jax
import jax.numpy as jnp
from jax import lax

L = 64
NCLS = 4
SUB = 32
NX = 128
NY = 1024


def draw_vertical_inverse(key, part):
    first_key, second_key = jax.random.split(jax.random.fold_in(key, 11))
    diagonal = jax.random.uniform(first_key, (NCLS, L), jnp.float32, 0.6, 1.0)
    spread = 0.06
    offdiag = spread * jax.random.normal(second_key, (NCLS, L, L), jnp.float32)
    return offdiag + jnp.eye(L, dtype=jnp.float32)[None] * diagonal[:, :, None]


def touch_ends(result, own_key, least, top_value):
    index_at = [jax.random.randint(jax.random.fold_in(own_key, axis), (), 0, length) for axis, length in enumerate(result.shape)]
    main_axis = result.shape.index(max(result.shape))
    beside = index_at[:main_axis] + [(index_at[main_axis] + 1) % result.shape[main_axis]] + index_at[main_axis + 1:]
    return result.at[tuple(index_at)].set(least).at[tuple(beside)].set(top_value)


def block_levels(own_key, shape, pieces, least, largest):
    def one(dim, shards_of):
        draws = jax.random.uniform(jax.random.fold_in(jax.random.fold_in(own_key, 6), dim), (shards_of,), jnp.float32, least / len(pieces), largest / len(pieces))
        return jnp.repeat(jnp.exp(draws), shape[dim] // shards_of).reshape((-1,) + (1,) * (len(shape) - dim - 1))

    level = one(*pieces[0])
    for cut in pieces[1:]:
        level = level * one(*cut)
    return level


def centred(key, extent, deviation, reach, pieces=(), held_as=jnp.bfloat16):
    gain = block_levels(key, extent, pieces, -0.22, 0.18) if pieces else 1.0
    array = jax.random.normal(key, extent, jnp.float32) * deviation * gain
    return jnp.minimum(jnp.maximum(array, -reach), reach).astype(held_as)


def setup_inputs(seed: int = 0) -> dict:
    streams_of = jax.random.split(jax.random.key(seed), 6)
    state = centred(streams_of[0], (4, L, NX, NY), 1.0, 6.0, ((2, 4), (3, 8)), jnp.float32)
    depth_class = touch_ends(jax.random.randint(streams_of[1], (NX, NY), 0, NCLS + 1), jax.random.fold_in(streams_of[1], 1), 0, NCLS).astype(jnp.int32)
    vertical_inverse = draw_vertical_inverse(jax.random.fold_in(streams_of[5], 71), 0)
    height = centred(streams_of[3], (NX, NY), 0.5, 4.0, ((0, 4), (1, 8)), jnp.float32)
    transport = centred(streams_of[4], (2, NX, NY), 0.5, 4.0, ((1, 4), (2, 8)), jnp.float32)
    return dict(state=state, depth_class=depth_class, vertical_inverse=vertical_inverse, height=height, transport=transport)


THERMAL = 0.8
HALINE = 0.6
PRESSURE_SCALE = 4.0
VISCOSITY = 0.1
STEP_TIME = 0.05
WAVE_STEP = 0.5
GRAVITY = 1.0
BOTTOM_DRAG = 0.05
CORIOLIS_BASE = 0.3
CORIOLIS_SLOPE = 0.4


def x_fourth(values):
    return (8.0 * (values[..., 3:-1, 2:-2] - values[..., 1:-3, 2:-2]) - (values[..., 4:, 2:-2] - values[..., :-4, 2:-2])) / 12.0


def y_fourth(values):
    return (8.0 * (values[..., 2:-2, 3:-1] - values[..., 2:-2, 1:-3]) - (values[..., 2:-2, 4:] - values[..., 2:-2, :-4])) / 12.0


def laplace(values):
    center = values[..., 2:-2, 2:-2]
    return values[..., 3:-1, 2:-2] + values[..., 1:-3, 2:-2] + values[..., 2:-2, 3:-1] + values[..., 2:-2, 1:-3] - 4.0 * center


def coriolis_row(anchor, number, total):
    position = (anchor + lax.broadcasted_iota(jnp.int32, (number,), 0)).astype(jnp.float32)
    return (CORIOLIS_BASE + CORIOLIS_SLOPE * (position + 0.5) / total)[None, :]


def baroclinic(state, padded, pressure, active, depth_class, inverse, coriolis):
    levels = state.shape[1]
    center = padded[:, :, 2:-2, 2:-2]
    east_vel = center[2]
    north_vel = center[3]
    tendency = -(east_vel * x_fourth(padded) + north_vel * y_fourth(padded)) + VISCOSITY * laplace(padded)
    zeros_field = jnp.zeros_like(east_vel)
    extra = jnp.stack([zeros_field, zeros_field, -x_fourth(pressure) + coriolis * north_vel, -y_fourth(pressure) - coriolis * east_vel])
    tendency = tendency + extra
    provisional = active * (center + STEP_TIME * tendency)
    solved = jnp.zeros_like(provisional)
    for class_index in range(inverse.shape[0]):
        chosen = (depth_class == class_index + 1).astype(jnp.float32)
        solved = solved + chosen * jnp.einsum('kl,flxy->fkxy', inverse[class_index], provisional, precision=lax.Precision.HIGHEST)
    updated = active * solved + (1.0 - active) * state
    forcing = jnp.sum(active * tendency[2:4], axis=1) / levels
    return updated, forcing


def shrink(values):
    return values[..., 1:-1, 1:-1]


def x_slope(values):
    return (values[2:, 1:-1] - values[:-2, 1:-1]) * 0.5


def y_slope(values):
    return (values[1:-1, 2:] - values[1:-1, :-2]) * 0.5


def substep(moving, fixed_fields, coriolis):
    surface, east_flow, north_flow = moving[0], moving[1], moving[2]
    column_depth = fixed_fields[2]
    sea_mask = (column_depth > 0.0).astype(jnp.float32)
    surface_mid = shrink(sea_mask) * (shrink(surface) - WAVE_STEP * (x_slope(east_flow) + y_slope(north_flow)))
    sea_inner = shrink(shrink(sea_mask))
    depth_inner = shrink(shrink(column_depth))
    force_east = shrink(shrink(fixed_fields[0]))
    force_north = shrink(shrink(fixed_fields[1]))
    coriolis_inner = coriolis[:, 2:-2]
    east_old = shrink(shrink(east_flow))
    north_old = shrink(shrink(north_flow))
    east_new = sea_inner * (east_old + WAVE_STEP * (-GRAVITY * depth_inner * x_slope(surface_mid) + coriolis_inner * north_old + force_east - BOTTOM_DRAG * east_old))
    north_new = sea_inner * (north_old + WAVE_STEP * (-GRAVITY * depth_inner * y_slope(surface_mid) - coriolis_inner * east_new + force_north - BOTTOM_DRAG * north_old))
    return jnp.stack([shrink(surface_mid), east_new, north_new])


def finish(updated, waves, active, depth_class, level_block, levels):
    counted = jnp.maximum(depth_class * level_block, 1).astype(jnp.float32)
    safe_depth = jnp.maximum(depth_class, 1).astype(jnp.float32) * level_block / levels
    column_means = jnp.sum(active * updated[2:4], axis=1) / counted
    carried = waves[1:3] / safe_depth
    velocity = updated[2:4] + active * (carried - column_means)[:, None]
    return jnp.concatenate([updated[0:2], velocity], axis=0)


def reference(state, depth_class, vertical_inverse, height, transport):
    levels = L
    level_block = L // NCLS
    level_ids = lax.broadcasted_iota(jnp.int32, (levels, 1, 1), 0)
    active = (level_ids < depth_class[None] * level_block).astype(jnp.float32)
    masked = state * active[None]
    padded = jnp.pad(masked, ((0, 0), (0, 0), (2, 2), (2, 2)))
    density = -THERMAL * padded[0] + HALINE * padded[1]
    pressure = (PRESSURE_SCALE / levels) * jnp.cumsum(density, axis=0)
    coriolis = coriolis_row(0, NY, NY)[0]
    updated, forcing = baroclinic(state, padded, pressure, active, depth_class, vertical_inverse, coriolis)
    column_depth = depth_class.astype(jnp.float32) * level_block / levels
    sea_mask = (depth_class > 0).astype(jnp.float32)
    moving = jnp.stack([height, transport[0], transport[1]]) * sea_mask
    fixed_fields = jnp.pad(jnp.stack([forcing[0], forcing[1], column_depth]), ((0, 0), (2, 2), (2, 2)))
    coriolis_wide = coriolis_row(-2, NY + 4, NY)

    def turn(index, current):
        return substep(jnp.pad(current, ((0, 0), (2, 2), (2, 2))), fixed_fields, coriolis_wide)

    waves = lax.fori_loop(0, SUB, turn, moving)
    state_next = finish(updated, waves, active, depth_class, level_block, levels)
    return state_next, waves[0], waves[1:3]
```

```python
import functools

import jax
import jax.numpy as jnp
from jax import lax
from jax.experimental import pallas as pl
from jax.experimental.pallas import tpu as pltpu
from jax.sharding import PartitionSpec as P

SUB = 32
THERMAL = 0.8
HALINE = 0.6
PRESSURE_SCALE = 4.0
VISCOSITY = 0.1
STEP_TIME = 0.05
BOTTOM_DRAG = 0.05
CORIOLIS_BASE = 0.3
CORIOLIS_SLOPE = 0.4
MESH = pl.DeviceIdType.MESH
OFFSETS = [(dx, dy) for dx in (1, -1, 2, -2, 0) for dy in (0, 1, -1) if (dx, dy) != (0, 0)]


def step_kernel(
    gxn, gyn, mdn,
    state_hbm, cls_ref, inv_ref, height_ref, transport_ref,
    upd_hbm, waves_ref, corr_ref,
    raw, mq, prov, updv, packed, from_left, from_right,
    win, fwin, wl, fo, flow, cons, nat, mean,
    raw_sem, out_sem, x_send, x_recv, y_send, y_recv, w_send, w_recv, f_send, f_recv,
):
    levels = inv_ref.shape[1]
    classes = inv_ref.shape[0]
    block = levels // classes
    rows = cls_ref.shape[0]
    cols = cls_ref.shape[1]
    span = win.shape[2]
    strips = span // 8
    blocks = span // rows
    gx = lax.axis_index("gx")
    yy = lax.axis_index("gy") * mdn + lax.axis_index("mode")
    yn = gyn * mdn
    ny = cols * yn

    def slot_of(dx):
        return (gx + dx) if blocks == gxn else (dx + 2)

    def inside(dx, dy):
        return (gx + dx >= 0) & (gx + dx < gxn) & (yy + dy >= 0) & (yy + dy < yn)

    def device(dx, dy):
        y2 = yy + dy
        return (gx + dx, y2 // mdn, lax.rem(y2, mdn))

    offsets = [o for o in OFFSETS if abs(o[0]) < gxn and abs(o[1]) < yn]

    loads = [pltpu.make_async_copy(state_hbm.at[f], raw.at[f], raw_sem.at[f]) for f in range(4)]
    for c in loads:
        c.start()

    win[...] = jnp.zeros_like(win)
    fwin[...] = jnp.zeros_like(fwin)
    cls = cls_ref[...]
    sea = (cls > 0).astype(jnp.float32)

    def own(ref):
        return ref.at[:, pl.ds(pl.multiple_of(slot_of(0) * rows, rows), rows), :]

    mine = own(win.at[0])
    mine[0] = cls.astype(jnp.float32)
    mine[1] = sea * height_ref[...]
    mine[2] = sea * transport_ref[0]
    mine[3] = sea * transport_ref[1]

    @pl.when(gx == 0)
    def _():
        mq[:, 0:2] = jnp.zeros((4, 2, levels, cols), jnp.float32)

    @pl.when(gx == gxn - 1)
    def _():
        mq[:, rows + 2 : rows + 4] = jnp.zeros((4, 2, levels, cols), jnp.float32)

    @pl.when(yy == 0)
    def _():
        from_left[...] = jnp.zeros_like(from_left)

    @pl.when(yy == yn - 1)
    def _():
        from_right[...] = jnp.zeros_like(from_right)

    barrier = pltpu.get_barrier_semaphore()
    total = 0
    for dx, dy in offsets:
        ok = inside(dx, dy)
        total = total + ok.astype(jnp.int32)

        @pl.when(ok)
        def _(dx=dx, dy=dy):
            pl.semaphore_signal(barrier, inc=1, device_id=device(dx, dy), device_id_type=MESH)

    pl.semaphore_wait(barrier, total)
    for c in loads:
        c.wait()

    level_block = lax.broadcasted_iota(jnp.int32, (levels, cols), 0) // block
    lane_full = lax.broadcasted_iota(jnp.int32, (levels, cols), 1)
    lane = lax.broadcasted_iota(jnp.int32, (8, cols), 1)
    sub = lax.broadcasted_iota(jnp.int32, (8, cols), 0)

    def mask_column(x):
        act = level_block < cls_ref[pl.ds(x, 1), :]
        spot = (lane_full >= 4 * x) & (lane_full < 4 * x + 4)
        shift = lax.rem(4 * x + 2, cols)
        for f in range(4):
            v = jnp.where(act, raw[f, pl.ds(x, levels, stride=rows), :], 0.0)
            mq[f, x + 2] = v
            packed[f] = jnp.where(spot, pltpu.roll(v, shift, 1), packed[f])

    packed[...] = jnp.zeros_like(packed)

    def edge_columns(work):
        def at(e, carry):
            work(jnp.where(e < 2, e, rows - 4 + e))
            return carry

        lax.fori_loop(0, 4, at, 0)

    def inner_columns(work):
        def at(x, carry):
            work(x)
            return carry

        lax.fori_loop(2, rows - 2, at, 0)

    edge_columns(mask_column)

    def x_copy(way):
        src, dst = (mq.at[:, 2:4], mq.at[:, rows + 2 : rows + 4]) if way < 0 else (
            mq.at[:, rows : rows + 2], mq.at[:, 0:2])
        i = 0 if way < 0 else 1
        return pltpu.make_async_remote_copy(
            src_ref=src, dst_ref=dst, send_sem=x_send.at[i], recv_sem=x_recv.at[i],
            device_id=device(way, 0), device_id_type=MESH)

    def y_copy(way):
        dst = from_right if way < 0 else from_left
        i = 0 if way < 0 else 1
        return pltpu.make_async_remote_copy(
            src_ref=packed, dst_ref=dst, send_sem=y_send.at[i], recv_sem=y_recv.at[i],
            device_id=device(0, way), device_id_type=MESH)

    def window_copy(ref, k, send, recv, arriving):
        dx, dy = offsets[k]
        side = {0: 0, 1: 1, -1: 2}[dy]
        if arriving:
            slot = slot_of(-dx)
        elif blocks == gxn:
            slot = gx
        else:
            slot = 2 - dx
        dst = ref.at[side, :, pl.ds(pl.multiple_of(slot * rows, rows), rows), :]
        return pltpu.make_async_remote_copy(
            src_ref=own(ref.at[0]), dst_ref=dst, send_sem=send.at[k], recv_sem=recv.at[k],
            device_id=device(-dx, -dy) if arriving else device(dx, dy), device_id_type=MESH)

    for way in (-1, 1):
        @pl.when(inside(way, 0))
        def _(way=way):
            x_copy(way).start()

    inner_columns(mask_column)
    for way in (-1, 1):
        @pl.when(inside(0, way))
        def _(way=way):
            y_copy(way).start()

    for k, (dx, dy) in enumerate(offsets):
        @pl.when(inside(dx, dy))
        def _(k=k):
            window_copy(win, k, w_send, w_recv, False).start()

    start = 0
    for c in range(classes):
        part = inv_ref[c][: block * (c + 1), :]
        high = part.astype(jnp.bfloat16)
        low = (part - high.astype(jnp.float32)).astype(jnp.bfloat16)
        wl[start : start + block * (c + 1), :] = jnp.concatenate([high, high, low], axis=1)
        start += block * (c + 1)

    for way in (-1, 1):
        @pl.when(inside(0, -way))
        def _(way=way):
            y_copy(way).wait_recv()

    slot_left = lax.rem(lane, 4) < 2
    position = (yy * cols + lane).astype(jnp.float32)
    coriolis = CORIOLIS_BASE + CORIOLIS_SLOPE * (position + 0.5) / ny

    def tendency_column(x):
        cls_row = cls_ref[pl.ds(x, 1), :]
        shift = lax.rem(2 * cols - 2 - 4 * x, cols)
        sum_east = jnp.zeros((8, cols), jnp.float32)
        sum_north = jnp.zeros((8, cols), jnp.float32)
        carry_x = jnp.zeros((1, cols), jnp.float32)
        carry_y = jnp.zeros((1, cols), jnp.float32)
        for l0 in range(0, levels, 8):
            act = jnp.broadcast_to((cls_row > l0 // block).astype(jnp.float32), (8, cols))
            u = mq[2, x + 2, l0 : l0 + 8, :]
            v = mq[3, x + 2, l0 : l0 + 8, :]
            u12 = u * (1.0 / 12.0)
            v12 = v * (1.0 / 12.0)
            density_x = density_y = None
            for f in range(4):
                c = mq[f, x + 2, l0 : l0 + 8, :]
                xm1 = mq[f, x + 1, l0 : l0 + 8, :]
                xp1 = mq[f, x + 3, l0 : l0 + 8, :]
                xm2 = mq[f, x, l0 : l0 + 8, :]
                xp2 = mq[f, x + 4, l0 : l0 + 8, :]
                h = jnp.where(slot_left, from_left[f, l0 : l0 + 8, :], from_right[f, l0 : l0 + 8, :])
                h = pltpu.roll(h, shift, 1)
                yp1 = pltpu.roll(jnp.where(lane < 1, h, c), cols - 1, 1)
                yp2 = pltpu.roll(jnp.where(lane < 2, h, c), cols - 2, 1)
                ym1 = pltpu.roll(jnp.where(lane > cols - 2, h, c), 1, 1)
                ym2 = pltpu.roll(jnp.where(lane > cols - 3, h, c), 2, 1)
                x12 = 8.0 * (xp1 - xm1) - (xp2 - xm2)
                y12 = 8.0 * (yp1 - ym1) - (yp2 - ym2)
                lap = (xp1 + xm1) + (yp1 + ym1) - 4.0 * c
                t = VISCOSITY * lap - (u12 * x12 + v12 * y12)
                if f == 0:
                    density_x, density_y = -THERMAL * x12, -THERMAL * y12
                elif f == 1:
                    gx_, gy_ = density_x + HALINE * x12, density_y + HALINE * y12
                    for k in (1, 2, 4):
                        gx_ = gx_ + jnp.where(sub >= k, pltpu.roll(gx_, k, 0), 0.0)
                        gy_ = gy_ + jnp.where(sub >= k, pltpu.roll(gy_, k, 0), 0.0)
                    gx_ = gx_ + carry_x
                    gy_ = gy_ + carry_y
                    carry_x, carry_y = gx_[7:8, :], gy_[7:8, :]
                elif f == 2:
                    t = t - (PRESSURE_SCALE / levels / 12.0) * gx_ + coriolis * v
                    sum_east = sum_east + act * t
                else:
                    t = t - (PRESSURE_SCALE / levels / 12.0) * gy_ - coriolis * u
                    sum_north = sum_north + act * t
                prov[x, f, l0 : l0 + 8, :] = act * (c + STEP_TIME * t)
        fo[0, pl.ds(x, 1), :] = jnp.sum(sum_east, axis=0, keepdims=True) * (1.0 / levels)
        fo[1, pl.ds(x, 1), :] = jnp.sum(sum_north, axis=0, keepdims=True) * (1.0 / levels)

    inner_columns(tendency_column)
    for way in (-1, 1):
        @pl.when(inside(-way, 0))
        def _(way=way):
            x_copy(way).wait_recv()

    edge_columns(tendency_column)

    mine_f = own(fwin.at[0])
    mine_f[0] = fo[0]
    mine_f[1] = fo[1]
    for k, (dx, dy) in enumerate(offsets):
        @pl.when(inside(dx, dy))
        def _(k=k):
            window_copy(fwin, k, f_send, f_recv, False).start()

    starts = [block * c * (c + 1) // 2 for c in range(classes)]

    def solve_column(x, carry):
        cls_row = cls_ref[pl.ds(x, 1), :]
        for pair in (0, 2):
            p = jnp.concatenate([prov[x, pair], prov[x, pair + 1]], axis=1)
            high = p.astype(jnp.bfloat16)
            low = (p - high.astype(jnp.float32)).astype(jnp.bfloat16)
            o = jnp.dot(
                wl[...], jnp.concatenate([high, low, high], axis=0),
                preferred_element_type=jnp.float32)
            for g in range(2):
                f = pair + g
                total_f = jnp.zeros((block, cols), jnp.float32)
                for b in range(classes):
                    picked = None
                    for c in range(b, classes):
                        r = starts[c] + block * b
                        piece = o[r : r + block, g * cols : (g + 1) * cols]
                        picked = piece if picked is None else jnp.where(cls_row == c + 1, piece, picked)
                    where = pl.ds(x + block * b * rows, block, stride=rows)
                    updv[f, where, :] = jnp.where(cls_row > b, picked, raw[f, where, :])
                    total_f = total_f + jnp.where(cls_row > b, picked, 0.0)
                if f >= 2:
                    mean[f - 2, pl.ds(x, 1), :] = jnp.sum(total_f, axis=0, keepdims=True)
        return carry

    lax.fori_loop(0, rows, solve_column, 0)
    stores = [pltpu.make_async_copy(updv.at[f], upd_hbm.at[f], out_sem.at[f]) for f in range(4)]
    for c in stores:
        c.start()

    for k, (dx, dy) in enumerate(offsets):
        @pl.when(inside(-dx, -dy))
        def _(k=k):
            window_copy(win, k, w_send, w_recv, True).wait_recv()
            window_copy(fwin, k, f_send, f_recv, True).wait_recv()

    half = lane < cols // 2
    place = [yy * cols + lane, yy * cols + jnp.where(half, lane + cols, lane - cols)]
    turn = [0.5 * (CORIOLIS_BASE + CORIOLIS_SLOPE * (p.astype(jnp.float32) + 0.5) / ny) for p in place]

    def strip(ref, i, j):
        at = pl.ds(i, 8, stride=strips)
        a = ref[0, j, at, :]
        return a, jnp.where(half, ref[2, j, at, :], ref[1, j, at, :])

    for i in range(strips):
        c = strip(win, i, 0)
        fields = [strip(win, i, 1 + j) for j in range(3)]
        f0, f1 = strip(fwin, i, 0), strip(fwin, i, 1)
        for t in range(2):
            wet = (c[t] > 0.0).astype(jnp.float32)
            cons[0, t, i] = 0.25 * wet
            cons[1, t, i] = c[t] * (0.25 * block / levels)
            cons[2, t, i] = 0.5 * wet * f0[t]
            cons[3, t, i] = 0.5 * wet * f1[t]
            for j in range(3):
                flow[j, t, i + 1] = fields[j][t]

    def edges(j):
        for t in range(2):
            flow[j, t, 0] = jnp.where(sub >= 1, pltpu.roll(flow[j, t, strips], 1, 0), 0.0)
            flow[j, t, strips + 1] = jnp.where(sub < 7, pltpu.roll(flow[j, t, 1], 7, 0), 0.0)

    first, last = lane == 0, lane == cols - 1

    def y_difference(a, b):
        ap, bp = pltpu.roll(a, cols - 1, 1), pltpu.roll(b, cols - 1, 1)
        am, bm = pltpu.roll(a, 1, 1), pltpu.roll(b, 1, 1)
        return (
            jnp.where(last, bp, ap) - jnp.where(first, bm, am),
            jnp.where(last, ap, bp) - jnp.where(first, am, bm),
        )

    edges(1)
    keep = 1.0 - 0.5 * BOTTOM_DRAG

    def substep(step, carry):
        for i in range(1, strips + 1):
            dy = y_difference(flow[2, 0, i], flow[2, 1, i])
            for t in range(2):
                dx = flow[1, t, i + 1] - flow[1, t, i - 1]
                flow[0, t, i] = flow[0, t, i] - cons[0, t, i - 1] * (dx + dy[t])
        edges(0)
        for i in range(1, strips + 1):
            dy = y_difference(flow[0, 0, i], flow[0, 1, i])
            for t in range(2):
                dx = flow[0, t, i + 1] - flow[0, t, i - 1]
                east, north, depth = flow[1, t, i], flow[2, t, i], cons[1, t, i - 1]
                east = (keep * east + turn[t] * north) + (cons[2, t, i - 1] - depth * dx)
                flow[1, t, i] = east
                flow[2, t, i] = (keep * north - turn[t] * east) + (cons[3, t, i - 1] - depth * dy[t])
        edges(1)
        return carry

    lax.fori_loop(0, SUB, substep, 0)

    for j in range(3):
        for i in range(strips):
            nat[j, pl.ds(i, 8, stride=strips), :] = flow[j, 0, i + 1]
    final = own(nat)
    for j in range(3):
        waves_ref[j] = final[j]
    counted = jnp.maximum(cls * block, 1).astype(jnp.float32)
    depth = jnp.maximum(cls, 1).astype(jnp.float32) * block / levels
    for j in range(2):
        corr_ref[j] = final[1 + j] / depth - mean[j] / counted

    for c in stores:
        c.wait()
    for way in (-1, 1):
        @pl.when(inside(way, 0))
        def _(way=way):
            x_copy(way).wait_send()

        @pl.when(inside(0, way))
        def _(way=way):
            y_copy(way).wait_send()
    for k, (dx, dy) in enumerate(offsets):
        @pl.when(inside(dx, dy))
        def _(k=k):
            window_copy(win, k, w_send, w_recv, False).wait_send()
            window_copy(fwin, k, f_send, f_recv, False).wait_send()


def finish_kernel(block, upd_ref, cls_ref, corr_ref, out_ref):
    cls = cls_ref[...]
    depth = pl.program_id(0)
    rows = cls.shape[0]
    out_ref[0:2] = upd_ref[0:2]
    for j in range(2):
        add = jnp.where(cls > depth, corr_ref[j], 0.0)
        for k in range(block):
            out_ref[2 + j, k * rows : (k + 1) * rows] = upd_ref[2 + j, k * rows : (k + 1) * rows] + add


def body(gxn, gyn, mdn, state, depth_class, vertical_inverse, height, transport):
    _, levels, rows, cols = state.shape
    classes = vertical_inverse.shape[0]
    block = levels // classes
    span = rows * min(5, gxn)
    strips = span // 8
    f32 = jnp.float32
    vmem = pl.BlockSpec(memory_space=pltpu.VMEM)
    hbm = pl.BlockSpec(memory_space=pl.ANY)
    k = len(OFFSETS)
    dma = pltpu.SemaphoreType.DMA
    wide = block * classes * (classes + 1) // 2
    flat = state.reshape(4, levels * rows, cols)
    upd, waves, corr = pl.pallas_call(
        functools.partial(step_kernel, gxn, gyn, mdn),
        out_shape=(
            jax.ShapeDtypeStruct(flat.shape, f32),
            jax.ShapeDtypeStruct((3, rows, cols), f32),
            jax.ShapeDtypeStruct((2, rows, cols), f32),
        ),
        in_specs=[hbm, vmem, vmem, vmem, vmem],
        out_specs=(hbm, vmem, vmem),
        scratch_shapes=[
            pltpu.VMEM((4, levels * rows, cols), f32),
            pltpu.VMEM((4, rows + 4, levels, cols), f32),
            pltpu.VMEM((rows, 4, levels, cols), f32),
            pltpu.VMEM((4, levels * rows, cols), f32),
            pltpu.VMEM((4, levels, cols), f32),
            pltpu.VMEM((4, levels, cols), f32),
            pltpu.VMEM((4, levels, cols), f32),
            pltpu.VMEM((3, 4, span, cols), f32),
            pltpu.VMEM((3, 2, span, cols), f32),
            pltpu.VMEM((wide, 3 * levels), jnp.bfloat16),
            pltpu.VMEM((2, rows, cols), f32),
            pltpu.VMEM((3, 2, strips + 2, 8, cols), f32),
            pltpu.VMEM((4, 2, strips, 8, cols), f32),
            pltpu.VMEM((3, span, cols), f32),
            pltpu.VMEM((2, rows, cols), f32),
            dma((4,)), dma((4,)), dma((2,)), dma((2,)), dma((2,)), dma((2,)),
            dma((k,)), dma((k,)), dma((k,)), dma((k,)),
        ],
        compiler_params=pltpu.CompilerParams(
            collective_id=0, has_side_effects=True, vmem_limit_bytes=48 * 2**20),
        cost_estimate=pl.CostEstimate(flops=10**9, bytes_accessed=2**23, transcendentals=0),
    )(flat, depth_class, vertical_inverse, height, transport)
    out = pl.pallas_call(
        functools.partial(finish_kernel, block),
        grid=(classes,),
        out_shape=jax.ShapeDtypeStruct(flat.shape, f32),
        in_specs=[
            pl.BlockSpec((4, block * rows, cols), lambda i: (0, i, 0)),
            pl.BlockSpec((rows, cols), lambda i: (0, 0)),
            pl.BlockSpec((2, rows, cols), lambda i: (0, 0, 0)),
        ],
        out_specs=pl.BlockSpec((4, block * rows, cols), lambda i: (0, i, 0)),
        compiler_params=pltpu.CompilerParams(vmem_limit_bytes=24 * 2**20),
        cost_estimate=pl.CostEstimate(flops=2**20, bytes_accessed=2**23, transcendentals=0),
    )(upd, depth_class, corr)
    return out.reshape(state.shape), waves[0], waves[1:3]


def solution(mesh):
    placed = (
        P(None, None, "gx", ("gy", "mode")),
        P("gx", ("gy", "mode")),
        P(),
        P("gx", ("gy", "mode")),
        P(None, "gx", ("gy", "mode")),
    )
    sizes = mesh.shape
    return jax.shard_map(
        functools.partial(body, sizes["gx"], sizes["gy"], sizes["mode"]),
        mesh=mesh,
        in_specs=placed,
        out_specs=(
            P(None, None, "gx", ("gy", "mode")),
            P("gx", ("gy", "mode")),
            P(None, "gx", ("gy", "mode")),
        ),
        check_vma=False,
    )
```

```python
import functools

import jax
import jax.numpy as jnp
from jax import lax
from jax.experimental import pallas as pl
from jax.experimental.pallas import tpu as pltpu
from jax.sharding import PartitionSpec as P

SUB = 32
THERMAL = 0.8
HALINE = 0.6
PRESSURE_SCALE = 4.0
VISCOSITY = 0.1
STEP_TIME = 0.05
BOTTOM_DRAG = 0.05
CORIOLIS_BASE = 0.3
CORIOLIS_SLOPE = 0.4
MESH = pl.DeviceIdType.MESH
STEPS = (1, -1, 2, -2)


def step_kernel(
    gxn, gyn, mdn,
    state_hbm, cls_hbm, inv_hbm, height_hbm, transport_hbm,
    upd_ref, small_ref,
    raw, cls_ref, inv_ref, height_ref, transport_ref,
    mq, prov, packed, from_left, from_right,
    win, fwin, win_out, win_left, win_right, fwin_out, fwin_left, fwin_right,
    win_side, fwin_side, wl, fo, flow, cons, nat, mean,
    raw_sem, in_sem, x_send, x_recv, y_send, y_recv,
    w_send, w_recv, f_send, f_recv, wy_send, wy_recv, fy_send, fy_recv,
):
    levels = inv_ref.shape[1]
    classes = inv_ref.shape[0]
    block = levels // classes
    rows = cls_ref.shape[0]
    cols = cls_ref.shape[1]
    span = win.shape[1]
    strips = span // 8
    blocks = span // rows
    gx = lax.axis_index("gx")
    yy = lax.axis_index("gy") * mdn + lax.axis_index("mode")
    yn = gyn * mdn
    ny = cols * yn

    def slot_of(dx):
        return (gx + dx) if blocks == gxn else (dx + 2)

    def inside(dx, dy):
        return (gx + dx >= 0) & (gx + dx < gxn) & (yy + dy >= 0) & (yy + dy < yn)

    def device(dx, dy):
        y2 = yy + dy
        return (gx + dx, y2 // mdn, lax.rem(y2, mdn))

    steps = [dx for dx in STEPS if abs(dx) < gxn]

    small = [
        pltpu.make_async_copy(a, b, in_sem.at[i])
        for i, (a, b) in enumerate((
            (cls_hbm, cls_ref), (height_hbm, height_ref), (transport_hbm, transport_ref), (inv_hbm, inv_ref)))
    ]
    for c in small:
        c.start()
    loads = [pltpu.make_async_copy(state_hbm.at[f], raw.at[f], raw_sem.at[f]) for f in range(4)]
    for c in loads:
        c.start()

    win[...] = jnp.zeros_like(win)
    fwin[...] = jnp.zeros_like(fwin)
    for c in small[:3]:
        c.wait()
    cls = cls_ref[...]
    sea = (cls > 0).astype(jnp.float32)

    def own(ref):
        return ref.at[:, pl.ds(pl.multiple_of(slot_of(0) * rows, rows), rows), :]

    mine = own(win)
    mine[0] = cls.astype(jnp.float32)
    mine[1] = sea * height_ref[...]
    mine[2] = sea * transport_ref[0]
    mine[3] = sea * transport_ref[1]

    @pl.when(gx == 0)
    def _():
        mq[:, 0:2] = jnp.zeros((4, 2, levels, cols), jnp.float32)

    @pl.when(gx == gxn - 1)
    def _():
        mq[:, rows + 2 : rows + 4] = jnp.zeros((4, 2, levels, cols), jnp.float32)

    @pl.when(yy == 0)
    def _():
        from_left[...] = jnp.zeros_like(from_left)
        win_left[...] = jnp.zeros_like(win_left)
        fwin_left[...] = jnp.zeros_like(fwin_left)

    @pl.when(yy == yn - 1)
    def _():
        from_right[...] = jnp.zeros_like(from_right)
        win_right[...] = jnp.zeros_like(win_right)
        fwin_right[...] = jnp.zeros_like(fwin_right)

    barrier = pltpu.get_barrier_semaphore()
    total = 0
    for dx, dy in [(d, 0) for d in steps] + [(0, 1), (0, -1)]:
        ok = inside(dx, dy)
        total = total + ok.astype(jnp.int32)

        @pl.when(ok)
        def _(dx=dx, dy=dy):
            pl.semaphore_signal(barrier, inc=1, device_id=device(dx, dy), device_id_type=MESH)

    pl.semaphore_wait(barrier, total)
    for c in loads:
        c.wait()

    level_block = lax.broadcasted_iota(jnp.int32, (levels, cols), 0) // block
    lane_full = lax.broadcasted_iota(jnp.int32, (levels, cols), 1)
    lane = lax.broadcasted_iota(jnp.int32, (8, cols), 1)
    sub = lax.broadcasted_iota(jnp.int32, (8, cols), 0)

    def mask_column(x):
        act = level_block < cls_ref[pl.ds(x, 1), :]
        spot = (lane_full >= 4 * x) & (lane_full < 4 * x + 4)
        shift = lax.rem(4 * x + 2, cols)
        for f in range(4):
            v = jnp.where(act, raw[f, pl.ds(x, levels, stride=rows), :], 0.0)
            mq[f, x + 2] = v
            packed[f] = jnp.where(spot, pltpu.roll(v, shift, 1), packed[f])

    packed[...] = jnp.zeros_like(packed)

    def edge_columns(work):
        def at(e, carry):
            work(jnp.where(e < 2, e, rows - 4 + e))
            return carry

        lax.fori_loop(0, 4, at, 0)

    def inner_columns(work):
        def at(x, carry):
            work(x)
            return carry

        lax.fori_loop(2, rows - 2, at, 0)

    edge_columns(mask_column)

    def x_copy(way):
        src, dst = (mq.at[:, 2:4], mq.at[:, rows + 2 : rows + 4]) if way < 0 else (
            mq.at[:, rows : rows + 2], mq.at[:, 0:2])
        i = 0 if way < 0 else 1
        return pltpu.make_async_remote_copy(
            src_ref=src, dst_ref=dst, send_sem=x_send.at[i], recv_sem=x_recv.at[i],
            device_id=device(way, 0), device_id_type=MESH)

    def y_copy(way):
        dst = from_right if way < 0 else from_left
        i = 0 if way < 0 else 1
        return pltpu.make_async_remote_copy(
            src_ref=packed, dst_ref=dst, send_sem=y_send.at[i], recv_sem=y_recv.at[i],
            device_id=device(0, way), device_id_type=MESH)

    def window_copy(ref, k, send, recv, arriving):
        dx = steps[k]
        if arriving:
            slot = slot_of(-dx)
        elif blocks == gxn:
            slot = gx
        else:
            slot = 2 - dx
        dst = ref.at[:, pl.ds(pl.multiple_of(slot * rows, rows), rows), :]
        return pltpu.make_async_remote_copy(
            src_ref=own(ref), dst_ref=dst, send_sem=send.at[k], recv_sem=recv.at[k],
            device_id=device(-dx if arriving else dx, 0), device_id_type=MESH)

    def window_y_copy(out, left, right, send, recv, way):
        i = 0 if way < 0 else 1
        return pltpu.make_async_remote_copy(
            src_ref=out.at[i], dst_ref=right if way < 0 else left,
            send_sem=send.at[i], recv_sem=recv.at[i],
            device_id=device(0, way), device_id_type=MESH)

    win_y = functools.partial(window_y_copy, win_out, win_left, win_right, wy_send, wy_recv)
    fwin_y = functools.partial(window_y_copy, fwin_out, fwin_left, fwin_right, fy_send, fy_recv)
    wide_half = lax.broadcasted_iota(jnp.int32, (span // 2, cols), 1) < cols // 2

    def pass_on(ref, out, send, recv, copy):
        for k, dx in enumerate(steps):
            @pl.when(inside(-dx, 0))
            def _(k=k):
                window_copy(ref, k, send, recv, True).wait_recv()

        for j in range(ref.shape[0]):
            top, low = ref[j, : span // 2], ref[j, span // 2 :]
            out[0, j] = jnp.where(wide_half, top, pltpu.roll(low, cols // 2, 1))
            out[1, j] = jnp.where(wide_half, pltpu.roll(top, cols // 2, 1), low)
        for way in (-1, 1):
            @pl.when(inside(0, way))
            def _(way=way):
                copy(way).start()

    def take_sides(ref, left, right, copy, side):
        for way in (-1, 1):
            @pl.when(inside(0, -way))
            def _(way=way):
                copy(way).wait_recv()

        for j in range(ref.shape[0]):
            l, r = left[j], right[j]
            side[j, : span // 2] = jnp.where(wide_half, r, pltpu.roll(l, cols // 2, 1))
            side[j, span // 2 :] = jnp.where(wide_half, pltpu.roll(r, cols // 2, 1), l)

    for way in (-1, 1):
        @pl.when(inside(way, 0))
        def _(way=way):
            x_copy(way).start()

    inner_columns(mask_column)
    for way in (-1, 1):
        @pl.when(inside(0, way))
        def _(way=way):
            y_copy(way).start()

    small[3].wait()
    start = 0
    for c in range(classes):
        part = inv_ref[c][: block * (c + 1), :]
        high = part.astype(jnp.bfloat16)
        low = (part - high.astype(jnp.float32)).astype(jnp.bfloat16)
        wl[start : start + block * (c + 1), :] = jnp.concatenate([high, high, low], axis=1)
        start += block * (c + 1)

    for way in (-1, 1):
        @pl.when(inside(0, -way))
        def _(way=way):
            y_copy(way).wait_recv()

    slot_left = lax.rem(lane, 4) < 2
    position = (yy * cols + lane).astype(jnp.float32)
    coriolis = CORIOLIS_BASE + CORIOLIS_SLOPE * (position + 0.5) / ny

    def tendency_column(x):
        cls_row = cls_ref[pl.ds(x, 1), :]
        shift = lax.rem(2 * cols - 2 - 4 * x, cols)
        sum_east = jnp.zeros((8, cols), jnp.float32)
        sum_north = jnp.zeros((8, cols), jnp.float32)
        carry_x = jnp.zeros((1, cols), jnp.float32)
        carry_y = jnp.zeros((1, cols), jnp.float32)
        for l0 in range(0, levels, 8):
            act = jnp.broadcast_to((cls_row > l0 // block).astype(jnp.float32), (8, cols))
            u = mq[2, x + 2, l0 : l0 + 8, :]
            v = mq[3, x + 2, l0 : l0 + 8, :]
            u12 = u * (1.0 / 12.0)
            v12 = v * (1.0 / 12.0)
            density_x = density_y = None
            for f in range(4):
                c = mq[f, x + 2, l0 : l0 + 8, :]
                xm1 = mq[f, x + 1, l0 : l0 + 8, :]
                xp1 = mq[f, x + 3, l0 : l0 + 8, :]
                xm2 = mq[f, x, l0 : l0 + 8, :]
                xp2 = mq[f, x + 4, l0 : l0 + 8, :]
                h = jnp.where(slot_left, from_left[f, l0 : l0 + 8, :], from_right[f, l0 : l0 + 8, :])
                h = pltpu.roll(h, shift, 1)
                yp1 = pltpu.roll(jnp.where(lane < 1, h, c), cols - 1, 1)
                yp2 = pltpu.roll(jnp.where(lane < 2, h, c), cols - 2, 1)
                ym1 = pltpu.roll(jnp.where(lane > cols - 2, h, c), 1, 1)
                ym2 = pltpu.roll(jnp.where(lane > cols - 3, h, c), 2, 1)
                x12 = 8.0 * (xp1 - xm1) - (xp2 - xm2)
                y12 = 8.0 * (yp1 - ym1) - (yp2 - ym2)
                lap = (xp1 + xm1) + (yp1 + ym1) - 4.0 * c
                t = VISCOSITY * lap - (u12 * x12 + v12 * y12)
                if f == 0:
                    density_x, density_y = -THERMAL * x12, -THERMAL * y12
                elif f == 1:
                    gx_, gy_ = density_x + HALINE * x12, density_y + HALINE * y12
                    for k in (1, 2, 4):
                        gx_ = gx_ + jnp.where(sub >= k, pltpu.roll(gx_, k, 0), 0.0)
                        gy_ = gy_ + jnp.where(sub >= k, pltpu.roll(gy_, k, 0), 0.0)
                    gx_ = gx_ + carry_x
                    gy_ = gy_ + carry_y
                    carry_x, carry_y = gx_[7:8, :], gy_[7:8, :]
                elif f == 2:
                    t = t - (PRESSURE_SCALE / levels / 12.0) * gx_ + coriolis * v
                    sum_east = sum_east + act * t
                else:
                    t = t - (PRESSURE_SCALE / levels / 12.0) * gy_ - coriolis * u
                    sum_north = sum_north + act * t
                prov[x, f, l0 : l0 + 8, :] = act * (c + STEP_TIME * t)
        fo[0, pl.ds(x, 1), :] = jnp.sum(sum_east, axis=0, keepdims=True) * (1.0 / levels)
        fo[1, pl.ds(x, 1), :] = jnp.sum(sum_north, axis=0, keepdims=True) * (1.0 / levels)

    starts = [block * c * (c + 1) // 2 for c in range(classes)]

    def solve_column(x):
        cls_row = cls_ref[pl.ds(x, 1), :]
        for pair in (0, 2):
            p = jnp.concatenate([prov[x, pair], prov[x, pair + 1]], axis=1)
            high = p.astype(jnp.bfloat16)
            low = (p - high.astype(jnp.float32)).astype(jnp.bfloat16)
            o = jnp.dot(
                wl[...], jnp.concatenate([high, low, high], axis=0),
                preferred_element_type=jnp.float32)
            for g in range(2):
                f = pair + g
                total_f = jnp.zeros((block, cols), jnp.float32)
                for b in range(classes):
                    picked = None
                    for c in range(b, classes):
                        r = starts[c] + block * b
                        piece = o[r : r + block, g * cols : (g + 1) * cols]
                        picked = piece if picked is None else jnp.where(cls_row == c + 1, piece, picked)
                    where = pl.ds(x + block * b * rows, block, stride=rows)
                    upd_ref[f, where, :] = jnp.where(cls_row > b, picked, raw[f, where, :])
                    total_f = total_f + jnp.where(cls_row > b, picked, 0.0)
                if f >= 2:
                    mean[f - 2, pl.ds(x, 1), :] = jnp.sum(total_f, axis=0, keepdims=True)

    def solve_columns(first, last):
        def at(x, carry):
            solve_column(x)
            return carry

        lax.fori_loop(first, last, at, 0)

    inner_columns(tendency_column)
    for way in (-1, 1):
        @pl.when(inside(-way, 0))
        def _(way=way):
            x_copy(way).wait_recv()

    edge_columns(tendency_column)

    mine_f = own(fwin)
    mine_f[0] = fo[0]
    mine_f[1] = fo[1]
    for k, dx in enumerate(steps):
        @pl.when(inside(dx, 0))
        def _(k=k):
            window_copy(fwin, k, f_send, f_recv, False).start()

    for k, dx in enumerate(steps):
        @pl.when(inside(dx, 0))
        def _(k=k):
            window_copy(win, k, w_send, w_recv, False).start()

    solve_columns(0, rows // 2)
    pass_on(fwin, fwin_out, f_send, f_recv, fwin_y)
    pass_on(win, win_out, w_send, w_recv, win_y)
    solve_columns(rows // 2, rows)
    take_sides(win, win_left, win_right, win_y, win_side)
    take_sides(fwin, fwin_left, fwin_right, fwin_y, fwin_side)

    half = lane < cols // 2
    place = [yy * cols + lane, yy * cols + jnp.where(half, lane + cols, lane - cols)]
    turn = [0.5 * (CORIOLIS_BASE + CORIOLIS_SLOPE * (p.astype(jnp.float32) + 0.5) / ny) for p in place]

    def strip(refs, i, j):
        at = pl.ds(i, 8, stride=strips)
        return refs[0][j, at, :], refs[1][j, at, :]

    wins, fwins = (win, win_side), (fwin, fwin_side)

    for i in range(strips):
        c = strip(wins, i, 0)
        fields = [strip(wins, i, 1 + j) for j in range(3)]
        f0, f1 = strip(fwins, i, 0), strip(fwins, i, 1)
        for t in range(2):
            wet = (c[t] > 0.0).astype(jnp.float32)
            cons[0, t, i] = 0.25 * wet
            cons[1, t, i] = c[t] * (0.25 * block / levels)
            cons[2, t, i] = 0.5 * wet * f0[t]
            cons[3, t, i] = 0.5 * wet * f1[t]
            for j in range(3):
                flow[j, t, i + 1] = fields[j][t]

    def edges(j):
        for t in range(2):
            flow[j, t, 0] = jnp.where(sub >= 1, pltpu.roll(flow[j, t, strips], 1, 0), 0.0)
            flow[j, t, strips + 1] = jnp.where(sub < 7, pltpu.roll(flow[j, t, 1], 7, 0), 0.0)

    first, last = lane == 0, lane == cols - 1

    def y_difference(a, b):
        ap, bp = pltpu.roll(a, cols - 1, 1), pltpu.roll(b, cols - 1, 1)
        am, bm = pltpu.roll(a, 1, 1), pltpu.roll(b, 1, 1)
        return (
            jnp.where(last, bp, ap) - jnp.where(first, bm, am),
            jnp.where(last, ap, bp) - jnp.where(first, am, bm),
        )

    edges(1)
    keep = 1.0 - 0.5 * BOTTOM_DRAG

    def substep(step, carry):
        for i in range(1, strips + 1):
            dy = y_difference(flow[2, 0, i], flow[2, 1, i])
            for t in range(2):
                dx = flow[1, t, i + 1] - flow[1, t, i - 1]
                flow[0, t, i] = flow[0, t, i] - cons[0, t, i - 1] * (dx + dy[t])
        edges(0)
        for i in range(1, strips + 1):
            dy = y_difference(flow[0, 0, i], flow[0, 1, i])
            for t in range(2):
                dx = flow[0, t, i + 1] - flow[0, t, i - 1]
                east, north, depth = flow[1, t, i], flow[2, t, i], cons[1, t, i - 1]
                east = (keep * east + turn[t] * north) + (cons[2, t, i - 1] - depth * dx)
                flow[1, t, i] = east
                flow[2, t, i] = (keep * north - turn[t] * east) + (cons[3, t, i - 1] - depth * dy[t])
        edges(1)
        return carry

    lax.fori_loop(0, SUB, substep, 0)

    for j in range(3):
        for i in range(strips):
            nat[j, pl.ds(i, 8, stride=strips), :] = flow[j, 0, i + 1]
    final = own(nat)
    for j in range(3):
        small_ref[j] = final[j]
    counted = jnp.maximum(cls * block, 1).astype(jnp.float32)
    depth = jnp.maximum(cls, 1).astype(jnp.float32) * block / levels
    for j in range(2):
        small_ref[3 + j] = final[1 + j] / depth - mean[j] / counted

    small_ref[5] = cls.astype(jnp.float32)

    for way in (-1, 1):
        @pl.when(inside(way, 0))
        def _(way=way):
            x_copy(way).wait_send()

        @pl.when(inside(0, way))
        def _(way=way):
            y_copy(way).wait_send()
            win_y(way).wait_send()
            fwin_y(way).wait_send()
    for k, dx in enumerate(steps):
        @pl.when(inside(dx, 0))
        def _(k=k):
            window_copy(win, k, w_send, w_recv, False).wait_send()
            window_copy(fwin, k, f_send, f_recv, False).wait_send()


def finish_kernel(block, upd_ref, small_ref, out_hbm, height_ref, transport_ref, velocity, sem):
    cls = small_ref[5]
    rows = cls.shape[0]
    piece = block * rows
    copies = [pltpu.make_async_copy(upd_ref.at[f], out_hbm.at[f], sem.at[f]) for f in range(2)]
    for c in copies:
        c.start()
    for depth in range(upd_ref.shape[1] // piece):
        for j in range(2):
            add = jnp.where(cls > depth, small_ref[3 + j], 0.0)
            for k in range(block):
                at = slice(depth * piece + k * rows, depth * piece + (k + 1) * rows)
                velocity[j, at] = upd_ref[2 + j, at] + add
            at = pl.ds(depth * piece, piece)
            copies.append(pltpu.make_async_copy(
                velocity.at[j, at], out_hbm.at[2 + j, at], sem.at[2 + 2 * depth + j]))
            copies[-1].start()
    height_ref[...] = small_ref[0]
    transport_ref[...] = small_ref[1:3]
    for c in copies:
        c.wait()


def body(gxn, gyn, mdn, state, depth_class, vertical_inverse, height, transport):
    _, levels, rows, cols = state.shape
    classes = vertical_inverse.shape[0]
    block = levels // classes
    span = rows * min(5, gxn)
    strips = span // 8
    f32 = jnp.float32
    vmem = pl.BlockSpec(memory_space=pltpu.VMEM)
    hbm = pl.BlockSpec(memory_space=pltpu.HBM)
    k = len(STEPS)
    dma = pltpu.SemaphoreType.DMA
    wide = block * classes * (classes + 1) // 2
    flat = state.reshape(4, levels * rows, cols)
    keep_in_hbm = [pltpu.with_memory_space_constraint(a, pltpu.HBM) for a in (depth_class, vertical_inverse, height, transport)]
    upd, small = pl.pallas_call(
        functools.partial(step_kernel, gxn, gyn, mdn),
        out_shape=(
            jax.ShapeDtypeStruct(flat.shape, f32),
            jax.ShapeDtypeStruct((6, rows, cols), f32),
        ),
        in_specs=[hbm] * 5,
        out_specs=(vmem, vmem),
        scratch_shapes=[
            pltpu.VMEM((4, levels * rows, cols), f32),
            pltpu.VMEM((rows, cols), jnp.int32),
            pltpu.VMEM(vertical_inverse.shape, f32),
            pltpu.VMEM((rows, cols), f32),
            pltpu.VMEM((2, rows, cols), f32),
            pltpu.VMEM((4, rows + 4, levels, cols), f32),
            pltpu.VMEM((rows, 4, levels, cols), f32),
            pltpu.VMEM((4, levels, cols), f32),
            pltpu.VMEM((4, levels, cols), f32),
            pltpu.VMEM((4, levels, cols), f32),
            pltpu.VMEM((4, span, cols), f32),
            pltpu.VMEM((2, span, cols), f32),
            pltpu.VMEM((2, 4, span // 2, cols), f32),
            pltpu.VMEM((4, span // 2, cols), f32),
            pltpu.VMEM((4, span // 2, cols), f32),
            pltpu.VMEM((2, 2, span // 2, cols), f32),
            pltpu.VMEM((2, span // 2, cols), f32),
            pltpu.VMEM((2, span // 2, cols), f32),
            pltpu.VMEM((4, span, cols), f32),
            pltpu.VMEM((2, span, cols), f32),
            pltpu.VMEM((wide, 3 * levels), jnp.bfloat16),
            pltpu.VMEM((2, rows, cols), f32),
            pltpu.VMEM((3, 2, strips + 2, 8, cols), f32),
            pltpu.VMEM((4, 2, strips, 8, cols), f32),
            pltpu.VMEM((3, span, cols), f32),
            pltpu.VMEM((2, rows, cols), f32),
            dma((4,)), dma((4,)), dma((2,)), dma((2,)), dma((2,)), dma((2,)),
            dma((k,)), dma((k,)), dma((k,)), dma((k,)), dma((2,)), dma((2,)), dma((2,)), dma((2,)),
        ],
        compiler_params=pltpu.CompilerParams(
            collective_id=0, has_side_effects=True, vmem_limit_bytes=48 * 2**20),
        cost_estimate=pl.CostEstimate(flops=10**9, bytes_accessed=2**23, transcendentals=0),
    )(flat, *keep_in_hbm)
    out, height_next, transport_next = pl.pallas_call(
        functools.partial(finish_kernel, block),
        out_shape=(
            jax.ShapeDtypeStruct(flat.shape, f32),
            jax.ShapeDtypeStruct((rows, cols), f32),
            jax.ShapeDtypeStruct((2, rows, cols), f32),
        ),
        in_specs=[vmem, vmem],
        out_specs=(pl.BlockSpec(memory_space=pl.ANY), vmem, vmem),
        scratch_shapes=[pltpu.VMEM((2, levels * rows, cols), f32), dma((2 + 2 * classes,))],
        compiler_params=pltpu.CompilerParams(vmem_limit_bytes=24 * 2**20),
        cost_estimate=pl.CostEstimate(flops=2**20, bytes_accessed=2**23, transcendentals=0),
    )(upd, small)
    return out.reshape(state.shape), height_next, transport_next


def solution(mesh):
    placed = (
        P(None, None, "gx", ("gy", "mode")),
        P("gx", ("gy", "mode")),
        P(),
        P("gx", ("gy", "mode")),
        P(None, "gx", ("gy", "mode")),
    )
    sizes = mesh.shape
    return jax.shard_map(
        functools.partial(body, sizes["gx"], sizes["gy"], sizes["mode"]),
        mesh=mesh,
        in_specs=placed,
        out_specs=(
            P(None, None, "gx", ("gy", "mode")),
            P("gx", ("gy", "mode")),
            P(None, "gx", ("gy", "mode")),
        ),
        check_vma=False,
    )
```

```python
import functools

import jax
import jax.numpy as jnp
from jax import lax
from jax.experimental import pallas as pl
from jax.experimental.pallas import tpu as pltpu
from jax.sharding import PartitionSpec as P

SUB = 32
THERMAL = 0.8
HALINE = 0.6
PRESSURE_SCALE = 4.0
VISCOSITY = 0.1
STEP_TIME = 0.05
BOTTOM_DRAG = 0.05
CORIOLIS_BASE = 0.3
CORIOLIS_SLOPE = 0.4
MESH = pl.DeviceIdType.MESH
STEPS = (1, -1, 2, -2)


def step_kernel(
    gxn, gyn, mdn,
    state_hbm, cls_hbm, inv_hbm, height_hbm, transport_hbm,
    upd_ref, small_ref,
    raw, cls_ref, inv_ref, height_ref, transport_ref,
    mq, prov, packed, from_left, from_right,
    win, fwin, win_out, win_left, win_right, fwin_out, fwin_left, fwin_right,
    win_side, fwin_side, wl, fo, flow, cons, nat, mean,
    raw_sem, in_sem, x_send, x_recv, y_send, y_recv,
    w_send, w_recv, f_send, f_recv, wy_send, wy_recv, fy_send, fy_recv,
):
    levels = inv_ref.shape[1]
    classes = inv_ref.shape[0]
    block = levels // classes
    rows = cls_ref.shape[0]
    cols = cls_ref.shape[1]
    span = win.shape[1]
    strips = span // 8
    blocks = span // rows
    gx = lax.axis_index("gx")
    yy = lax.axis_index("gy") * mdn + lax.axis_index("mode")
    yn = gyn * mdn
    ny = cols * yn

    def slot_of(dx):
        return (gx + dx) if blocks == gxn else (dx + 2)

    def inside(dx, dy):
        return (gx + dx >= 0) & (gx + dx < gxn) & (yy + dy >= 0) & (yy + dy < yn)

    def device(dx, dy):
        y2 = yy + dy
        return (gx + dx, y2 // mdn, lax.rem(y2, mdn))

    steps = [dx for dx in STEPS if abs(dx) < gxn]

    small = [
        pltpu.make_async_copy(a, b, in_sem.at[i])
        for i, (a, b) in enumerate((
            (cls_hbm, cls_ref), (height_hbm, height_ref), (transport_hbm, transport_ref), (inv_hbm, inv_ref)))
    ]
    for c in small:
        c.start()
    loads = [pltpu.make_async_copy(state_hbm.at[f], raw.at[f], raw_sem.at[f]) for f in range(4)]
    for c in loads:
        c.start()

    win[...] = jnp.zeros_like(win)
    fwin[...] = jnp.zeros_like(fwin)
    for c in small[:3]:
        c.wait()
    cls = cls_ref[...]
    sea = (cls > 0).astype(jnp.float32)

    def own(ref):
        return ref.at[:, pl.ds(pl.multiple_of(slot_of(0) * rows, rows), rows), :]

    mine = own(win)
    mine[0] = cls.astype(jnp.float32)
    mine[1] = sea * height_ref[...]
    mine[2] = sea * transport_ref[0]
    mine[3] = sea * transport_ref[1]

    @pl.when(gx == 0)
    def _():
        mq[:, 0:2] = jnp.zeros((4, 2, levels, cols), jnp.float32)

    @pl.when(gx == gxn - 1)
    def _():
        mq[:, rows + 2 : rows + 4] = jnp.zeros((4, 2, levels, cols), jnp.float32)

    @pl.when(yy == 0)
    def _():
        from_left[...] = jnp.zeros_like(from_left)
        win_left[...] = jnp.zeros_like(win_left)
        fwin_left[...] = jnp.zeros_like(fwin_left)

    @pl.when(yy == yn - 1)
    def _():
        from_right[...] = jnp.zeros_like(from_right)
        win_right[...] = jnp.zeros_like(win_right)
        fwin_right[...] = jnp.zeros_like(fwin_right)

    barrier = pltpu.get_barrier_semaphore()
    total = 0
    for dx, dy in [(d, 0) for d in steps] + [(0, 1), (0, -1)]:
        ok = inside(dx, dy)
        total = total + ok.astype(jnp.int32)

        @pl.when(ok)
        def _(dx=dx, dy=dy):
            pl.semaphore_signal(barrier, inc=1, device_id=device(dx, dy), device_id_type=MESH)

    pl.semaphore_wait(barrier, total)
    for c in loads:
        c.wait()

    level_block = lax.broadcasted_iota(jnp.int32, (levels, cols), 0) // block
    lane = lax.broadcasted_iota(jnp.int32, (8, cols), 1)
    sub = lax.broadcasted_iota(jnp.int32, (8, cols), 0)

    def mask_column(x):
        act = level_block < cls_ref[pl.ds(x, 1), :]
        for f in range(4):
            v = jnp.where(act, raw[f, pl.ds(x, levels, stride=rows), :], 0.0)
            mq[f, x + 2] = v

    def mask_levels(chunk, carry):
        depth = chunk // (block // 8)
        for f in range(4):
            lanes = jnp.zeros((8, cols), jnp.float32)
            for x in range(rows):
                v = raw[f, pl.ds(chunk * (8 * rows) + x, 8, stride=rows), :]
                v = jnp.where(cls_ref[x : x + 1, :] > depth, v, 0.0)
                at = pl.ds(pl.multiple_of(chunk * 8, 8), 8)
                if 2 <= x < rows - 2:
                    mq[f, x + 2, at, :] = v
                spot = (lane >= 4 * x) & (lane < 4 * x + 4)
                lanes = jnp.where(spot, pltpu.roll(v, (4 * x + 2) % cols, 1), lanes)
            packed[f, at, :] = lanes
        return carry


    def edge_columns(work):
        def at(e, carry):
            work(jnp.where(e < 2, e, rows - 4 + e))
            return carry

        lax.fori_loop(0, 4, at, 0)

    def inner_columns(work):
        def at(x, carry):
            work(x)
            return carry

        lax.fori_loop(2, rows - 2, at, 0)

    edge_columns(mask_column)

    def x_copy(way):
        src, dst = (mq.at[:, 2:4], mq.at[:, rows + 2 : rows + 4]) if way < 0 else (
            mq.at[:, rows : rows + 2], mq.at[:, 0:2])
        i = 0 if way < 0 else 1
        return pltpu.make_async_remote_copy(
            src_ref=src, dst_ref=dst, send_sem=x_send.at[i], recv_sem=x_recv.at[i],
            device_id=device(way, 0), device_id_type=MESH)

    def y_copy(way):
        dst = from_right if way < 0 else from_left
        i = 0 if way < 0 else 1
        return pltpu.make_async_remote_copy(
            src_ref=packed, dst_ref=dst, send_sem=y_send.at[i], recv_sem=y_recv.at[i],
            device_id=device(0, way), device_id_type=MESH)

    def window_copy(ref, k, send, recv, arriving):
        dx = steps[k]
        if arriving:
            slot = slot_of(-dx)
        elif blocks == gxn:
            slot = gx
        else:
            slot = 2 - dx
        dst = ref.at[:, pl.ds(pl.multiple_of(slot * rows, rows), rows), :]
        return pltpu.make_async_remote_copy(
            src_ref=own(ref), dst_ref=dst, send_sem=send.at[k], recv_sem=recv.at[k],
            device_id=device(-dx if arriving else dx, 0), device_id_type=MESH)

    def window_y_copy(out, left, right, send, recv, way):
        i = 0 if way < 0 else 1
        return pltpu.make_async_remote_copy(
            src_ref=out.at[i], dst_ref=right if way < 0 else left,
            send_sem=send.at[i], recv_sem=recv.at[i],
            device_id=device(0, way), device_id_type=MESH)

    win_y = functools.partial(window_y_copy, win_out, win_left, win_right, wy_send, wy_recv)
    fwin_y = functools.partial(window_y_copy, fwin_out, fwin_left, fwin_right, fy_send, fy_recv)
    wide_half = lax.broadcasted_iota(jnp.int32, (span // 2, cols), 1) < cols // 2

    def pass_on(ref, out, send, recv, copy):
        for k, dx in enumerate(steps):
            @pl.when(inside(-dx, 0))
            def _(k=k):
                window_copy(ref, k, send, recv, True).wait_recv()

        for j in range(ref.shape[0]):
            top, low = ref[j, : span // 2], ref[j, span // 2 :]
            out[0, j] = jnp.where(wide_half, top, pltpu.roll(low, cols // 2, 1))
            out[1, j] = jnp.where(wide_half, pltpu.roll(top, cols // 2, 1), low)
        for way in (-1, 1):
            @pl.when(inside(0, way))
            def _(way=way):
                copy(way).start()

    def take_sides(ref, left, right, copy, side):
        for way in (-1, 1):
            @pl.when(inside(0, -way))
            def _(way=way):
                copy(way).wait_recv()

        for j in range(ref.shape[0]):
            l, r = left[j], right[j]
            side[j, : span // 2] = jnp.where(wide_half, r, pltpu.roll(l, cols // 2, 1))
            side[j, span // 2 :] = jnp.where(wide_half, pltpu.roll(r, cols // 2, 1), l)

    for way in (-1, 1):
        @pl.when(inside(way, 0))
        def _(way=way):
            x_copy(way).start()

    lax.fori_loop(0, levels // 8, mask_levels, 0)
    for way in (-1, 1):
        @pl.when(inside(0, way))
        def _(way=way):
            y_copy(way).start()

    small[3].wait()
    start = 0
    for c in range(classes):
        part = inv_ref[c][: block * (c + 1), :]
        high = part.astype(jnp.bfloat16)
        low = (part - high.astype(jnp.float32)).astype(jnp.bfloat16)
        wl[start : start + block * (c + 1), :] = jnp.concatenate([high, high, low], axis=1)
        start += block * (c + 1)

    for way in (-1, 1):
        @pl.when(inside(0, -way))
        def _(way=way):
            y_copy(way).wait_recv()

    slot_left = lax.rem(lane, 4) < 2
    position = (yy * cols + lane).astype(jnp.float32)
    coriolis = CORIOLIS_BASE + CORIOLIS_SLOPE * (position + 0.5) / ny

    def tendency_column(x):
        cls_row = cls_ref[pl.ds(x, 1), :]
        shift = lax.rem(2 * cols - 2 - 4 * x, cols)
        sum_east = jnp.zeros((8, cols), jnp.float32)
        sum_north = jnp.zeros((8, cols), jnp.float32)
        carry_x = jnp.zeros((1, cols), jnp.float32)
        carry_y = jnp.zeros((1, cols), jnp.float32)
        for l0 in range(0, levels, 8):
            act = jnp.broadcast_to((cls_row > l0 // block).astype(jnp.float32), (8, cols))
            u = mq[2, x + 2, l0 : l0 + 8, :]
            v = mq[3, x + 2, l0 : l0 + 8, :]
            u12 = u * (1.0 / 12.0)
            v12 = v * (1.0 / 12.0)
            density_x = density_y = None
            for f in range(4):
                c = mq[f, x + 2, l0 : l0 + 8, :]
                xm1 = mq[f, x + 1, l0 : l0 + 8, :]
                xp1 = mq[f, x + 3, l0 : l0 + 8, :]
                xm2 = mq[f, x, l0 : l0 + 8, :]
                xp2 = mq[f, x + 4, l0 : l0 + 8, :]
                h = jnp.where(slot_left, from_left[f, l0 : l0 + 8, :], from_right[f, l0 : l0 + 8, :])
                h = pltpu.roll(h, shift, 1)
                yp1 = pltpu.roll(jnp.where(lane < 1, h, c), cols - 1, 1)
                yp2 = pltpu.roll(jnp.where(lane < 2, h, c), cols - 2, 1)
                ym1 = pltpu.roll(jnp.where(lane > cols - 2, h, c), 1, 1)
                ym2 = pltpu.roll(jnp.where(lane > cols - 3, h, c), 2, 1)
                x12 = 8.0 * (xp1 - xm1) - (xp2 - xm2)
                y12 = 8.0 * (yp1 - ym1) - (yp2 - ym2)
                lap = (xp1 + xm1) + (yp1 + ym1) - 4.0 * c
                t = VISCOSITY * lap - (u12 * x12 + v12 * y12)
                if f == 0:
                    density_x, density_y = -THERMAL * x12, -THERMAL * y12
                elif f == 1:
                    gx_, gy_ = density_x + HALINE * x12, density_y + HALINE * y12
                    for k in (1, 2, 4):
                        gx_ = gx_ + jnp.where(sub >= k, pltpu.roll(gx_, k, 0), 0.0)
                        gy_ = gy_ + jnp.where(sub >= k, pltpu.roll(gy_, k, 0), 0.0)
                    gx_ = gx_ + carry_x
                    gy_ = gy_ + carry_y
                    carry_x, carry_y = gx_[7:8, :], gy_[7:8, :]
                elif f == 2:
                    t = t - (PRESSURE_SCALE / levels / 12.0) * gx_ + coriolis * v
                    sum_east = sum_east + act * t
                else:
                    t = t - (PRESSURE_SCALE / levels / 12.0) * gy_ - coriolis * u
                    sum_north = sum_north + act * t
                prov[x, f, l0 : l0 + 8, :] = act * (c + STEP_TIME * t)
        fo[0, pl.ds(x, 1), :] = jnp.sum(sum_east, axis=0, keepdims=True) * (1.0 / levels)
        fo[1, pl.ds(x, 1), :] = jnp.sum(sum_north, axis=0, keepdims=True) * (1.0 / levels)

    starts = [block * c * (c + 1) // 2 for c in range(classes)]

    def solve_column(x):
        cls_row = cls_ref[pl.ds(x, 1), :]
        for pair in (0, 2):
            p = jnp.concatenate([prov[x, pair], prov[x, pair + 1]], axis=1)
            high = p.astype(jnp.bfloat16)
            low = (p - high.astype(jnp.float32)).astype(jnp.bfloat16)
            o = jnp.dot(
                wl[...], jnp.concatenate([high, low, high], axis=0),
                preferred_element_type=jnp.float32)
            for g in range(2):
                f = pair + g
                total_f = jnp.zeros((block, cols), jnp.float32)
                for b in range(classes):
                    picked = None
                    for c in range(b, classes):
                        r = starts[c] + block * b
                        piece = o[r : r + block, g * cols : (g + 1) * cols]
                        picked = piece if picked is None else jnp.where(cls_row == c + 1, piece, picked)
                    where = pl.ds(x + block * b * rows, block, stride=rows)
                    upd_ref[f, where, :] = jnp.where(cls_row > b, picked, raw[f, where, :])
                    total_f = total_f + jnp.where(cls_row > b, picked, 0.0)
                if f >= 2:
                    mean[f - 2, pl.ds(x, 1), :] = jnp.sum(total_f, axis=0, keepdims=True)

    def solve_columns(first, last):
        def at(x, carry):
            solve_column(x)
            return carry

        lax.fori_loop(first, last, at, 0, unroll=2)

    inner_columns(tendency_column)
    for way in (-1, 1):
        @pl.when(inside(-way, 0))
        def _(way=way):
            x_copy(way).wait_recv()

    edge_columns(tendency_column)

    mine_f = own(fwin)
    mine_f[0] = fo[0]
    mine_f[1] = fo[1]
    for k, dx in enumerate(steps):
        @pl.when(inside(dx, 0))
        def _(k=k):
            window_copy(fwin, k, f_send, f_recv, False).start()

    for k, dx in enumerate(steps):
        @pl.when(inside(dx, 0))
        def _(k=k):
            window_copy(win, k, w_send, w_recv, False).start()

    solve_columns(0, rows // 2)
    pass_on(fwin, fwin_out, f_send, f_recv, fwin_y)
    pass_on(win, win_out, w_send, w_recv, win_y)
    solve_columns(rows // 2, rows)
    take_sides(win, win_left, win_right, win_y, win_side)
    take_sides(fwin, fwin_left, fwin_right, fwin_y, fwin_side)

    half = lane < cols // 2
    place = [yy * cols + lane, yy * cols + jnp.where(half, lane + cols, lane - cols)]
    turn = [0.5 * (CORIOLIS_BASE + CORIOLIS_SLOPE * (p.astype(jnp.float32) + 0.5) / ny) for p in place]

    def strip(refs, i, j):
        at = pl.ds(i, 8, stride=strips)
        return refs[0][j, at, :], refs[1][j, at, :]

    wins, fwins = (win, win_side), (fwin, fwin_side)

    for i in range(strips):
        c = strip(wins, i, 0)
        fields = [strip(wins, i, 1 + j) for j in range(3)]
        f0, f1 = strip(fwins, i, 0), strip(fwins, i, 1)
        for t in range(2):
            wet = (c[t] > 0.0).astype(jnp.float32)
            cons[0, t, i] = 0.25 * wet
            cons[1, t, i] = c[t] * (0.25 * block / levels)
            cons[2, t, i] = 0.5 * wet * f0[t]
            cons[3, t, i] = 0.5 * wet * f1[t]
            for j in range(3):
                flow[j, t, i + 1] = fields[j][t]

    def edges(j):
        for t in range(2):
            flow[j, t, 0] = jnp.where(sub >= 1, pltpu.roll(flow[j, t, strips], 1, 0), 0.0)
            flow[j, t, strips + 1] = jnp.where(sub < 7, pltpu.roll(flow[j, t, 1], 7, 0), 0.0)

    first, last = lane == 0, lane == cols - 1

    def y_difference(a, b):
        ap, bp = pltpu.roll(a, cols - 1, 1), pltpu.roll(b, cols - 1, 1)
        am, bm = pltpu.roll(a, 1, 1), pltpu.roll(b, 1, 1)
        return (
            jnp.where(last, bp, ap) - jnp.where(first, bm, am),
            jnp.where(last, ap, bp) - jnp.where(first, am, bm),
        )

    edges(1)
    keep = 1.0 - 0.5 * BOTTOM_DRAG

    def substep(step, carry):
        for i in range(1, strips + 1):
            dy = y_difference(flow[2, 0, i], flow[2, 1, i])
            for t in range(2):
                dx = flow[1, t, i + 1] - flow[1, t, i - 1]
                flow[0, t, i] = flow[0, t, i] - cons[0, t, i - 1] * (dx + dy[t])
        edges(0)
        for i in range(1, strips + 1):
            dy = y_difference(flow[0, 0, i], flow[0, 1, i])
            for t in range(2):
                dx = flow[0, t, i + 1] - flow[0, t, i - 1]
                east, north, depth = flow[1, t, i], flow[2, t, i], cons[1, t, i - 1]
                east = (keep * east + turn[t] * north) + (cons[2, t, i - 1] - depth * dx)
                flow[1, t, i] = east
                flow[2, t, i] = (keep * north - turn[t] * east) + (cons[3, t, i - 1] - depth * dy[t])
        edges(1)
        return carry

    lax.fori_loop(0, SUB, substep, 0)

    for j in range(3):
        for i in range(strips):
            nat[j, pl.ds(i, 8, stride=strips), :] = flow[j, 0, i + 1]
    final = own(nat)
    for j in range(3):
        small_ref[j] = final[j]
    counted = jnp.maximum(cls * block, 1).astype(jnp.float32)
    depth = jnp.maximum(cls, 1).astype(jnp.float32) * block / levels
    for j in range(2):
        small_ref[3 + j] = final[1 + j] / depth - mean[j] / counted

    small_ref[5] = cls.astype(jnp.float32)

    for way in (-1, 1):
        @pl.when(inside(way, 0))
        def _(way=way):
            x_copy(way).wait_send()

        @pl.when(inside(0, way))
        def _(way=way):
            y_copy(way).wait_send()
            win_y(way).wait_send()
            fwin_y(way).wait_send()
    for k, dx in enumerate(steps):
        @pl.when(inside(dx, 0))
        def _(k=k):
            window_copy(win, k, w_send, w_recv, False).wait_send()
            window_copy(fwin, k, f_send, f_recv, False).wait_send()


def finish_kernel(block, upd_ref, small_ref, out_hbm, height_ref, transport_ref, velocity, sem):
    cls = small_ref[5]
    rows = cls.shape[0]
    piece = block * rows
    copies = [pltpu.make_async_copy(upd_ref.at[f], out_hbm.at[f], sem.at[f]) for f in range(2)]
    for c in copies:
        c.start()
    for depth in range(upd_ref.shape[1] // piece):
        for j in range(2):
            add = jnp.where(cls > depth, small_ref[3 + j], 0.0)
            for k in range(block):
                at = slice(depth * piece + k * rows, depth * piece + (k + 1) * rows)
                velocity[j, at] = upd_ref[2 + j, at] + add
            at = pl.ds(depth * piece, piece)
            copies.append(pltpu.make_async_copy(
                velocity.at[j, at], out_hbm.at[2 + j, at], sem.at[2 + 2 * depth + j]))
            copies[-1].start()
    height_ref[...] = small_ref[0]
    transport_ref[...] = small_ref[1:3]
    for c in copies:
        c.wait()


def body(gxn, gyn, mdn, state, depth_class, vertical_inverse, height, transport):
    _, levels, rows, cols = state.shape
    classes = vertical_inverse.shape[0]
    block = levels // classes
    span = rows * min(5, gxn)
    strips = span // 8
    f32 = jnp.float32
    vmem = pl.BlockSpec(memory_space=pltpu.VMEM)
    hbm = pl.BlockSpec(memory_space=pltpu.HBM)
    k = len(STEPS)
    dma = pltpu.SemaphoreType.DMA
    wide = block * classes * (classes + 1) // 2
    flat = state.reshape(4, levels * rows, cols)
    keep_in_hbm = [pltpu.with_memory_space_constraint(a, pltpu.HBM) for a in (depth_class, vertical_inverse, height, transport)]
    upd, small = pl.pallas_call(
        functools.partial(step_kernel, gxn, gyn, mdn),
        out_shape=(
            jax.ShapeDtypeStruct(flat.shape, f32),
            jax.ShapeDtypeStruct((6, rows, cols), f32),
        ),
        in_specs=[hbm] * 5,
        out_specs=(vmem, vmem),
        scratch_shapes=[
            pltpu.VMEM((4, levels * rows, cols), f32),
            pltpu.VMEM((rows, cols), jnp.int32),
            pltpu.VMEM(vertical_inverse.shape, f32),
            pltpu.VMEM((rows, cols), f32),
            pltpu.VMEM((2, rows, cols), f32),
            pltpu.VMEM((4, rows + 4, levels, cols), f32),
            pltpu.VMEM((rows, 4, levels, cols), f32),
            pltpu.VMEM((4, levels, cols), f32),
            pltpu.VMEM((4, levels, cols), f32),
            pltpu.VMEM((4, levels, cols), f32),
            pltpu.VMEM((4, span, cols), f32),
            pltpu.VMEM((2, span, cols), f32),
            pltpu.VMEM((2, 4, span // 2, cols), f32),
            pltpu.VMEM((4, span // 2, cols), f32),
            pltpu.VMEM((4, span // 2, cols), f32),
            pltpu.VMEM((2, 2, span // 2, cols), f32),
            pltpu.VMEM((2, span // 2, cols), f32),
            pltpu.VMEM((2, span // 2, cols), f32),
            pltpu.VMEM((4, span, cols), f32),
            pltpu.VMEM((2, span, cols), f32),
            pltpu.VMEM((wide, 3 * levels), jnp.bfloat16),
            pltpu.VMEM((2, rows, cols), f32),
            pltpu.VMEM((3, 2, strips + 2, 8, cols), f32),
            pltpu.VMEM((4, 2, strips, 8, cols), f32),
            pltpu.VMEM((3, span, cols), f32),
            pltpu.VMEM((2, rows, cols), f32),
            dma((4,)), dma((4,)), dma((2,)), dma((2,)), dma((2,)), dma((2,)),
            dma((k,)), dma((k,)), dma((k,)), dma((k,)), dma((2,)), dma((2,)), dma((2,)), dma((2,)),
        ],
        compiler_params=pltpu.CompilerParams(
            collective_id=0, has_side_effects=True, vmem_limit_bytes=48 * 2**20),
        cost_estimate=pl.CostEstimate(flops=10**9, bytes_accessed=2**23, transcendentals=0),
    )(flat, *keep_in_hbm)
    out, height_next, transport_next = pl.pallas_call(
        functools.partial(finish_kernel, block),
        out_shape=(
            jax.ShapeDtypeStruct(flat.shape, f32),
            jax.ShapeDtypeStruct((rows, cols), f32),
            jax.ShapeDtypeStruct((2, rows, cols), f32),
        ),
        in_specs=[vmem, vmem],
        out_specs=(pl.BlockSpec(memory_space=pl.ANY), vmem, vmem),
        scratch_shapes=[pltpu.VMEM((2, levels * rows, cols), f32), dma((2 + 2 * classes,))],
        compiler_params=pltpu.CompilerParams(vmem_limit_bytes=24 * 2**20),
        cost_estimate=pl.CostEstimate(flops=2**20, bytes_accessed=2**23, transcendentals=0),
    )(upd, small)
    return out.reshape(state.shape), height_next, transport_next


def solution(mesh):
    placed = (
        P(None, None, "gx", ("gy", "mode")),
        P("gx", ("gy", "mode")),
        P(),
        P("gx", ("gy", "mode")),
        P(None, "gx", ("gy", "mode")),
    )
    sizes = mesh.shape
    return jax.shard_map(
        functools.partial(body, sizes["gx"], sizes["gy"], sizes["mode"]),
        mesh=mesh,
        in_specs=placed,
        out_specs=(
            P(None, None, "gx", ("gy", "mode")),
            P("gx", ("gy", "mode")),
            P(None, "gx", ("gy", "mode")),
        ),
        check_vma=False,
    )
```
